32 devices in a mesh: seq: 16 (over z, y, core), head: 2 (over x).
Axes of the slice: x: 2, y: 2, z: 4, core: 2. Of those that a mesh axis runs over, the one named last changes fastest.
Arguments:
- tokens: bfloat16 [8192, 1024], P('seq', 'head'), may hold values from -6 to 6
- w_qkv: bfloat16 [1, 1024, 3, 1024], P(None, None, None, 'head'), may hold values from -0.1875 to 0.1875
- w_out: bfloat16 [1, 1024, 1024], P(None, 'head'), may hold values from -0.1875 to 0.1875
- gain_in: bfloat16 [1, 1024], replicated, may hold values from 0.099609375 to 1.8984375
- gain_mid: bfloat16 [1, 1024], P(None, 'head'), may hold values from 0.099609375 to 1.8984375
Outputs:
- hidden: bfloat16 [8192, 1024], P('seq', 'head')
The draws below stay inside these ranges and needn't reach their ends.
All inputs are finite; a program needn't handle non-finite values.
Results may differ from the reference program's by a relative error of at most 0.014.
Values may be sent and summed in bfloat16 or wider, within the bound.
A program may use at most 192 MiB of HBM per device.

```python
import math
import jax
import jax.numpy as jnp
from jax import lax

D = 1024
H = 16
DH = 64
LAYERS = 1
TOK_DEV = 512
FEAT = 2080
TOKENS = 8192
N_SEQ = 16


def block_levels(stream_key, extent, shards, low, largest):
    def one(axis_at, parts):
        heights = jax.random.uniform(jax.random.fold_in(jax.random.fold_in(stream_key, 6), axis_at), (parts,), jnp.float32, low / len(shards), largest / len(shards))
        return jnp.repeat(jnp.exp(heights), extent[axis_at] // parts).reshape((-1,) + (1,) * (len(extent) - axis_at - 1))

    level = one(*shards[0])
    for cut in shards[1:]:
        level = level * one(*cut)
    return level


def gaussian(key, shape, scale, most, cuts=(), kind=jnp.bfloat16):
    level = block_levels(key, shape, cuts, -0.22, 0.18) if cuts else 1.0
    entries = jax.random.normal(key, shape, jnp.float32) * scale * level
    return jnp.minimum(jnp.maximum(entries, -most), most).astype(kind)


def setup_inputs(seed: int = 0) -> dict:
    splits = jax.random.split(jax.random.key(seed), 6)
    return {
        "tokens": gaussian(splits[0], (TOKENS, D), 1.0, 6.0, ((0, 16), (1, 2))),
        "w_qkv": gaussian(splits[1], (LAYERS, D, 3, H * DH), D ** -0.5, 0.1875, ((3, 2),)),
        "w_out": gaussian(splits[2], (LAYERS, H * DH, D), (H * DH) ** -0.5, 0.1875, ((1, 2),)),
        "gain_in": jnp.clip(1.0 + 0.18 * jax.random.normal(splits[3], (LAYERS, D), jnp.float32), 0.099609375, 1.8984375).astype(jnp.bfloat16),
        "gain_mid": jnp.clip(1.0 + 0.18 * jax.random.normal(splits[4], (LAYERS, H * DH), jnp.float32), 0.099609375, 1.8984375).astype(jnp.bfloat16),
    }


EPSILON = 1e-06
SQRT_TWO = math.sqrt(2.0)

def expand(columns):
    pieces = []
    for column in range(columns.shape[1]):
        leading = columns[:, column:column + 1, :]
        pieces.append(leading * leading)
        pieces.append(SQRT_TWO * leading * columns[:, column + 1:, :])
    return jnp.concatenate(pieces, axis=1)

def highest_einsum(form, left, right):
    return jnp.einsum(form, left.astype(jnp.float32), right.astype(jnp.float32), precision=lax.Precision.HIGHEST)

def run_layer(hidden, weight_qkv, weight_out, gain_first, gain_second):
    blocks = hidden.reshape(N_SEQ, TOK_DEV, D)
    weight_heads = weight_qkv.reshape(D, 3, H, DH)
    row_ids = jnp.arange(TOK_DEV, dtype=jnp.int32)
    causal = row_ids[:, None] >= row_ids[None, :]

    def one_block(carry, block):
        prefix_state, prefix_norm = carry
        wide = block.astype(jnp.float32)
        normed = (wide * lax.rsqrt(lax.optimization_barrier(jnp.mean(wide * wide, axis=1, keepdims=True)) + EPSILON) * gain_first.astype(jnp.float32)).astype(jnp.bfloat16)
        projected = highest_einsum('td,dche->chet', normed, weight_heads).astype(jnp.bfloat16)
        query_cols, key_cols, value_cols = (projected[0], projected[1], projected[2])
        key_feats = expand(key_cols.astype(jnp.float32)).astype(jnp.bfloat16)
        query_feats = (expand(query_cols.astype(jnp.float32)) / DH).astype(jnp.bfloat16)
        scores = highest_einsum('hdt,hds->hts', query_cols, key_cols)
        weights = jnp.where(causal[None], scores * scores / DH, 0.0)
        local_den = lax.optimization_barrier(jnp.sum(weights, axis=2))
        local_num = highest_einsum('hts,hes->the', weights.astype(jnp.bfloat16), value_cols)
        num_prefix = highest_einsum('hft,hfe->the', query_feats, prefix_state.astype(jnp.bfloat16))
        den_prefix = highest_einsum('hft,hf->th', query_feats, prefix_norm.astype(jnp.bfloat16))
        attended = (local_num + num_prefix) / (1.0 + local_den.T + den_prefix)[:, :, None]
        attended = attended.reshape(TOK_DEV, H * DH)
        inverse_rms = lax.rsqrt(lax.optimization_barrier(jnp.mean(attended * attended, axis=1, keepdims=True)) + EPSILON)
        mixed_in = (attended * inverse_rms * gain_second.astype(jnp.float32)).astype(jnp.bfloat16)
        update = jnp.dot(mixed_in, weight_out, preferred_element_type=jnp.float32)
        new_block = (wide + update).astype(jnp.bfloat16)
        block_state = highest_einsum('hft,het->hfe', key_feats, value_cols)
        block_norm = lax.optimization_barrier(jnp.sum(key_feats.astype(jnp.float32), axis=2))
        return ((prefix_state + block_state, prefix_norm + block_norm), new_block)
    initial = (jnp.zeros((H, FEAT, DH), jnp.float32), jnp.zeros((H, FEAT), jnp.float32))
    final_carry, new_blocks = lax.scan(one_block, initial, blocks)
    return new_blocks.reshape(TOKENS, D)

def reference(tokens, w_qkv, w_out, gain_in, gain_mid):
    hidden = tokens
    for layer_index in range(LAYERS):
        hidden = run_layer(hidden, w_qkv[layer_index], w_out[layer_index], gain_in[layer_index], gain_mid[layer_index])
    return hidden
```

```python
import functools

import jax
import jax.numpy as jnp
from jax import lax
from jax.experimental import pallas as pl
from jax.experimental.pallas import tpu as pltpu
from jax.sharding import PartitionSpec as P

DH = 64
EPSILON = 1e-06
MESH = pl.DeviceIdType.MESH
OFFSETS = DH // 2 + 1
FEATS = OFFSETS * DH
ROWS = FEATS + DH
PARTS = 4


def dot(a, b, dims=((1,), (0,))):
    return lax.dot_general(a, b, (dims, ((), ())), preferred_element_type=jnp.float32)


def kernel(
    n, nx, x_ref, w_ref, wo_ref, gain_in_ref, gain_mid_ref, out_ref,
    xbuf, q_t, k_t, v_t, v_pair, feat, twice, state, prefix, outgoing, num, den, att, ss, part_out, part_in,
    x_send, x_recv, chain_send, chain_recv, ss_send, ss_recv, part_send, part_recv,
):
    me = lax.axis_index("seq")
    hx = lax.axis_index("head")
    rows, width = x_ref.shape
    features = w_ref.shape[2]
    heads = features // DH
    pairs = heads // 2
    full = nx * width
    piece = ROWS // PARTS
    right, left = lax.rem(me + 1, n), lax.rem(me + n - 1, n)

    barrier = pltpu.get_barrier_semaphore()
    for neighbour in (left, right):
        pl.semaphore_signal(barrier, inc=1, device_id=(neighbour, hx), device_id_type=MESH)
    for k in range(1, nx):
        pl.semaphore_signal(
            barrier, inc=1, device_id=(me, lax.rem(hx + k, nx)), device_id_type=MESH
        )
    pl.semaphore_wait(barrier, 2 + nx - 1)

    def token_copy(k):
        return pltpu.make_async_remote_copy(
            src_ref=x_ref, dst_ref=xbuf.at[hx], send_sem=x_send.at[k], recv_sem=x_recv.at[k],
            device_id=(me, lax.rem(hx + k, nx)), device_id_type=MESH,
        )

    for k in range(1, nx):
        token_copy(k).start()
    xbuf[hx] = x_ref[...]
    for k in range(1, nx):
        token_copy(k).wait()

    total = jnp.zeros((rows, 1), jnp.float32)
    for j in range(nx):
        wide = xbuf[j].astype(jnp.float32)
        total = total + jnp.sum(wide * wide, axis=1, keepdims=True)
    inverse = lax.rsqrt(total / full + EPSILON)
    for j in range(nx):
        gain = gain_in_ref[:, j * width:(j + 1) * width].astype(jnp.float32)
        xbuf[j] = (xbuf[j].astype(jnp.float32) * inverse * gain).astype(jnp.bfloat16)
    for c in range(3):
        y = dot(xbuf[0], w_ref[c, :width, :])
        for j in range(1, nx):
            y = y + dot(xbuf[j], w_ref[c, j * width:(j + 1) * width, :])
        y = y.astype(jnp.bfloat16)
        flipped = y.T.reshape(heads, DH, rows)
        (q_t, k_t, v_t)[c][...] = flipped
        if c == 2:
            for p in range(pairs):
                v_pair[p] = y[:, p * 2 * DH:(p + 1) * 2 * DH]

    low_lane = lax.broadcasted_iota(jnp.int32, (1, 2 * DH), 1) < DH

    def expand(u, edge, middle):
        wide = u.astype(jnp.float32)
        twice[:DH, :] = wide
        twice[DH:, :] = wide
        for d in range(OFFSETS):
            scaled = edge if d in (0, OFFSETS - 1) else middle
            feat[d * DH:(d + 1) * DH, :] = scaled * twice[d:d + DH, :].astype(jnp.bfloat16)

    def make_state(p):
        both = jnp.concatenate([k_t[2 * p], k_t[2 * p + 1]], axis=0)
        values = v_pair[p]
        for a in range(2):
            u = k_t[2 * p + a]
            expand(u, u, u)
            step = FEATS // PARTS
            for i in range(PARTS):
                at = slice(i * step, (i + 1) * step)
                got = dot(feat[at, :], values)
                state[p, at, :] = got if a == 0 else jnp.where(low_lane, state[p, at, :], got)
            gram = dot(u, both, ((1,), (1,)))
            at = slice(FEATS, ROWS)
            state[p, at, :] = gram if a == 0 else jnp.where(low_lane, state[p, at, :], gram)

    causal = lax.broadcasted_iota(jnp.int32, (rows, rows), 0) <= lax.broadcasted_iota(
        jnp.int32, (rows, rows), 1
    )

    def local(h, carry):
        scores = dot(k_t[h], q_t[h], ((0,), (0,)))
        weights = jnp.where(causal, scores * scores * (1.0 / DH), 0.0)
        den[h] = jnp.sum(weights, axis=0, keepdims=True)
        num[h] = dot(v_t[h], weights.astype(jnp.bfloat16))
        return carry

    def chain_copy(p, i):
        return pltpu.make_async_remote_copy(
            src_ref=outgoing.at[p, i], dst_ref=prefix.at[p, i],
            send_sem=chain_send.at[p, i], recv_sem=chain_recv.at[p, i],
            device_id=(right, hx), device_id_type=MESH,
        )

    @pl.when(me == 0)
    def _():
        prefix[...] = jnp.zeros_like(prefix)

    make_state(0)
    late = me >= n // 2
    lax.fori_loop(0, jnp.where(late, heads, 0), local, 0)

    def turn(p, carry):
        @pl.when(p + 1 < pairs)
        def _():
            make_state(p + 1)

        for i in range(PARTS):
            copy = chain_copy(p, i)

            @pl.when(me > 0)
            def _():
                copy.wait_recv()

            @pl.when(me < n - 1)
            def _():
                own = state[p, i * piece:(i + 1) * piece, :]
                outgoing[p, i] = (prefix[p, i].astype(jnp.float32) + own).astype(jnp.bfloat16)
                copy.start()

        whole = prefix[p].reshape(ROWS, 2 * DH).T
        for a in range(2):
            h = 2 * p + a
            u = q_t[h]
            expand(u, u * (1.0 / DH), u * (2.0 / DH))
            mine = whole[a * DH:(a + 1) * DH, :]
            num[h] = num[h] + dot(mine[:, :FEATS], feat[...])
            gram = dot(mine[:, FEATS:], u)
            den[h] = den[h] + jnp.sum(
                gram * u.astype(jnp.float32), axis=0, keepdims=True
            ) * (1.0 / DH)
        return carry

    @pl.when(jnp.logical_not(late))
    def _():
        num[...] = jnp.zeros_like(num)
        den[...] = jnp.zeros_like(den)

    lax.fori_loop(0, pairs, turn, 0)

    def late_local(h, carry):
        old_num, old_den = num[h], den[h]
        local(h, carry)
        num[h] = num[h] + old_num
        den[h] = den[h] + old_den
        return carry

    lax.fori_loop(0, jnp.where(late, 0, heads), late_local, 0)

    attended = (num[...] / (1.0 + den[...])).reshape(features, rows)
    ss[0] = jnp.broadcast_to(jnp.sum(attended * attended, axis=0, keepdims=True), (8, rows))

    def ss_copy(k):
        return pltpu.make_async_remote_copy(
            src_ref=ss.at[0], dst_ref=ss.at[k], send_sem=ss_send.at[k], recv_sem=ss_recv.at[k],
            device_id=(me, lax.rem(hx + k, nx)), device_id_type=MESH,
        )

    def part_copy(k):
        return pltpu.make_async_remote_copy(
            src_ref=part_out.at[k], dst_ref=part_in.at[k], send_sem=part_send.at[k],
            recv_sem=part_recv.at[k],
            device_id=(me, lax.rem(hx + k, nx)), device_id_type=MESH,
        )

    for k in range(1, nx):
        ss_copy(k).start()
    att[...] = (attended.T * gain_mid_ref[...].astype(jnp.float32)).astype(jnp.bfloat16)
    for k in range(1, nx):
        at = pl.multiple_of(lax.rem(hx + k, nx) * width, width)
        part_out[k] = dot(att[...], wo_ref[:, pl.ds(at, width)]).astype(jnp.bfloat16)
        part_copy(k).start()
    update = dot(att[...], wo_ref[:, pl.ds(pl.multiple_of(hx * width, width), width)])
    for k in range(1, nx):
        ss_copy(k).wait()
    squares = ss[0]
    for k in range(1, nx):
        squares = squares + ss[k]
    columns = jnp.broadcast_to(squares[:1], (128, rows)).T[:, :1]
    scale = lax.rsqrt(columns / full + EPSILON)
    for k in range(1, nx):
        part_copy(k).wait()
        update = update + part_in[k].astype(jnp.float32)
    out_ref[...] = (x_ref[...].astype(jnp.float32) + update * scale).astype(jnp.bfloat16)

    @pl.when(me < n - 1)
    def _():
        for p in range(pairs):
            for i in range(PARTS):
                chain_copy(p, i).wait_send()


def shards(n, nx, tokens, w_qkv, w_out, gain_in, gain_mid):
    rows, width = tokens.shape
    features = w_qkv.shape[3]
    heads = features // DH
    pairs = heads // 2
    bf16, f32 = jnp.bfloat16, jnp.float32
    dma = pltpu.SemaphoreType.DMA
    return pl.pallas_call(
        functools.partial(kernel, n, nx),
        out_shape=jax.ShapeDtypeStruct((rows, width), bf16),
        in_specs=[pl.BlockSpec(memory_space=pltpu.VMEM)] * 5,
        out_specs=pl.BlockSpec(memory_space=pltpu.VMEM),
        scratch_shapes=[
            pltpu.VMEM((nx, rows, width), bf16),
            pltpu.VMEM((heads, DH, rows), bf16),
            pltpu.VMEM((heads, DH, rows), bf16),
            pltpu.VMEM((heads, DH, rows), bf16),
            pltpu.VMEM((pairs, rows, 2 * DH), bf16),
            pltpu.VMEM((FEATS, rows), bf16),
            pltpu.VMEM((2 * DH, rows), f32),
            pltpu.VMEM((pairs, ROWS, 2 * DH), f32),
            pltpu.VMEM((pairs, PARTS, ROWS // PARTS, 2 * DH), bf16),
            pltpu.VMEM((pairs, PARTS, ROWS // PARTS, 2 * DH), bf16),
            pltpu.VMEM((heads, DH, rows), f32),
            pltpu.VMEM((heads, 1, rows), f32),
            pltpu.VMEM((rows, features), bf16),
            pltpu.VMEM((nx, 8, rows), f32),
            pltpu.VMEM((nx, rows, width), bf16),
            pltpu.VMEM((nx, rows, width), bf16),
            dma((nx,)), dma((nx,)),
            dma((pairs, PARTS)), dma((pairs, PARTS)),
            dma((nx,)), dma((nx,)),
            dma((nx,)), dma((nx,)),
        ],
        compiler_params=pltpu.CompilerParams(
            collective_id=0, has_side_effects=True, vmem_limit_bytes=48 * 1024 * 1024
        ),
    )(tokens, w_qkv[0].transpose(1, 0, 2), w_out[0], gain_in, gain_mid)


def solution(mesh):
    placed = (
        P("seq", "head"),
        P(None, None, None, "head"),
        P(None, "head", None),
        P(),
        P(None, "head"),
    )
    return jax.shard_map(
        functools.partial(shards, mesh.shape["seq"], mesh.shape["head"]),
        mesh=mesh, in_specs=placed, out_specs=P("seq", "head"), check_vma=False,
    )
```

```python
import functools

import jax
import jax.numpy as jnp
from jax import lax
from jax.experimental import pallas as pl
from jax.experimental.pallas import tpu as pltpu
from jax.sharding import PartitionSpec as P

DH = 64
EPSILON = 1e-06
MESH = pl.DeviceIdType.MESH
TILE = 16
FEATS = DH * (DH // 2 + 1)
ROWS = FEATS + DH
PARTS = 8


def dot(a, b, dims=((1,), (0,))):
    return lax.dot_general(a, b, (dims, ((), ())), preferred_element_type=jnp.float32)


def feature_tiles():
    tiles = []
    for r in range(TILE):
        for b in range(DH // TILE):
            for a in range(b + 1):
                if a < b or r <= TILE // 2:
                    tiles.append((a, b, r))
    return tiles


def kernel(
    n, nx, x_ref, w_hbm, wo_hbm, gain_in_ref, gain_mid_ref, out_ref,
    x_own, w_ref, wo_ref, wo_in, xbuf, q_t, k_t, v_t, v_pair, feat, twice, state, prefix, outgoing,
    num, den, att, att_in, ss,
    load_sem, x_send, x_recv, wo_send, wo_recv, chain_send, chain_recv, ss_send, ss_recv,
    att_send, att_recv,
):
    me = lax.axis_index("seq")
    hx = lax.axis_index("head")
    rows, width = x_own.shape
    features = w_ref.shape[2]
    heads = features // DH
    pairs = heads // 2
    full = nx * width
    piece = ROWS // PARTS
    right, left = lax.rem(me + 1, n), lax.rem(me + n - 1, n)

    def load(src, dst, i):
        return pltpu.make_async_copy(src, dst, load_sem.at[i])

    load(x_ref, x_own, 0).start()
    load(w_hbm, w_ref, 1).start()
    load(wo_hbm, wo_ref, 2).start()

    barrier = pltpu.get_barrier_semaphore()
    for neighbour in (left, right):
        pl.semaphore_signal(barrier, inc=1, device_id=(neighbour, hx), device_id_type=MESH)
    for k in range(1, nx):
        pl.semaphore_signal(
            barrier, inc=1, device_id=(me, lax.rem(hx + k, nx)), device_id_type=MESH
        )
    pl.semaphore_wait(barrier, 2 + nx - 1)

    def across(src, dst, send, recv, k):
        return pltpu.make_async_remote_copy(
            src_ref=src, dst_ref=dst, send_sem=send, recv_sem=recv,
            device_id=(me, lax.rem(hx + k, nx)), device_id_type=MESH,
        )

    def token_copy(k):
        return across(x_ref, xbuf.at[hx], x_send.at[k], x_recv.at[k], k)

    def wo_copy(k):
        at = pl.multiple_of(lax.rem(hx + k, nx) * width, width)
        return across(
            wo_ref.at[:, pl.ds(at, width)], wo_in.at[k], wo_send.at[k], wo_recv.at[k], k
        )

    def ss_copy(k):
        return across(ss.at[0], ss.at[k], ss_send.at[k], ss_recv.at[k], k)

    def att_copy(k, p):
        return across(att.at[p], att_in.at[k, p], att_send.at[k, p], att_recv.at[k, p], k)

    for k in range(1, nx):
        token_copy(k).start()

    num[...] = jnp.zeros_like(num)
    den[...] = jnp.zeros_like(den)
    ss[0] = jnp.zeros_like(ss[0])

    @pl.when(me == 0)
    def _():
        prefix[...] = jnp.zeros_like(prefix)

    load(x_ref, x_own, 0).wait()
    xbuf[hx] = x_own[...]
    load(w_hbm, w_ref, 1).wait()
    load(wo_hbm, wo_ref, 2).wait()
    for k in range(1, nx):
        token_copy(k).wait()
    for k in range(1, nx):
        wo_copy(k).start()

    total = jnp.zeros((rows, 1), jnp.float32)
    for j in range(nx):
        wide = xbuf[j].astype(jnp.float32)
        total = total + jnp.sum(wide * wide, axis=1, keepdims=True)
    inverse = lax.rsqrt(total / full + EPSILON)
    for j in range(nx):
        gain = gain_in_ref[:, j * width:(j + 1) * width].astype(jnp.float32)
        xbuf[j] = (xbuf[j].astype(jnp.float32) * inverse * gain).astype(jnp.bfloat16)

    def project(c):
        y = dot(xbuf[0], w_ref[c, :width, :])
        for j in range(1, nx):
            y = y + dot(xbuf[j], w_ref[c, j * width:(j + 1) * width, :])
        y = y.astype(jnp.bfloat16)
        (q_t, k_t, v_t)[c][...] = y.T.reshape(heads, DH, rows)
        if c == 2:
            for p in range(pairs):
                v_pair[p] = y[:, p * 2 * DH:(p + 1) * 2 * DH]

    low_lane = lax.broadcasted_iota(jnp.int32, (1, 2 * DH), 1) < DH
    tiles = feature_tiles()

    def expand(slot, u, edge, middle):
        wide = u.astype(jnp.float32)
        for j in range(rows // 128):
            lanes = slice(j * 128, (j + 1) * 128)
            for b in range(DH // TILE):
                tile = wide[b * TILE:(b + 1) * TILE, lanes]
                twice[slot, j, 2 * b * TILE:(2 * b + 1) * TILE, :] = tile
                twice[slot, j, (2 * b + 1) * TILE:(2 * b + 2) * TILE, :] = tile
        for j in range(rows // 128):
            lanes = slice(j * 128, (j + 1) * 128)
            rolled, held = None, None
            for at, (a, b, r) in enumerate(tiles):
                if held != (b, r):
                    low = 2 * b * TILE + r
                    rolled = twice[slot, j, low:low + TILE, :].astype(jnp.bfloat16)
                    held = (b, r)
                scaled = edge if a == b and r in (0, TILE // 2) else middle
                feat[slot, at * TILE:(at + 1) * TILE, lanes] = (
                    scaled[a * TILE:(a + 1) * TILE, lanes] * rolled
                )

    def make_state(p):
        both = jnp.concatenate([k_t[2 * p], k_t[2 * p + 1]], axis=0)
        values = v_pair[p]
        for a in range(2):
            u = k_t[2 * p + a]
            expand(a, u, u, u)
        step = FEATS // 4
        for i in range(4):
            at = slice(i * step, (i + 1) * step)
            state[p, at, :] = jnp.where(
                low_lane, dot(feat[0, at, :], values), dot(feat[1, at, :], values)
            )
        state[p, FEATS:, :] = jnp.where(
            low_lane, dot(k_t[2 * p], both, ((1,), (1,))), dot(k_t[2 * p + 1], both, ((1,), (1,)))
        )

    causal = lax.broadcasted_iota(jnp.int32, (rows, rows), 0) <= lax.broadcasted_iota(
        jnp.int32, (rows, rows), 1
    )

    def local(h, carry):
        scores = dot(k_t[h], q_t[h], ((0,), (0,)))
        weights = jnp.where(causal, scores * scores * (1.0 / DH), 0.0)
        den[h] = den[h] + jnp.sum(weights, axis=0, keepdims=True)
        num[h] = num[h] + dot(v_t[h], weights.astype(jnp.bfloat16))
        return carry

    def chain_copy(p, i):
        return pltpu.make_async_remote_copy(
            src_ref=outgoing.at[p, i], dst_ref=prefix.at[p, i],
            send_sem=chain_send.at[p, i], recv_sem=chain_recv.at[p, i],
            device_id=(right, hx), device_id_type=MESH,
        )

    def forward(p):
        for i in range(PARTS):
            copy = chain_copy(p, i)

            @pl.when(me > 0)
            def _():
                copy.wait_recv()

            @pl.when(me < n - 1)
            def _():
                own = state[p, i * piece:(i + 1) * piece, :]
                outgoing[p, i] = (prefix[p, i].astype(jnp.float32) + own).astype(jnp.bfloat16)
                copy.start()

    late = me >= n // 2
    early = jnp.logical_not(late)

    project(1)
    project(2)

    def first(p, carry):
        make_state(p)

        @pl.when(early)
        def _():
            forward(p)

        return carry

    lax.fori_loop(0, pairs, first, 0)
    project(0)
    lax.fori_loop(0, jnp.where(late, heads, 0), local, 0)

    def second(p, carry):
        @pl.when(late)
        def _():
            forward(p)

        whole = prefix[p].reshape(ROWS, 2 * DH).T
        for a in range(2):
            h = 2 * p + a
            u = q_t[h]
            expand(a, u, u * (1.0 / DH), u * (2.0 / DH))
            mine = whole[a * DH:(a + 1) * DH, :]
            num[h] = num[h] + dot(mine[:, :FEATS], feat[a])
            gram = dot(mine[:, FEATS:], u)
            den[h] = den[h] + jnp.sum(
                gram * u.astype(jnp.float32), axis=0, keepdims=True
            ) * (1.0 / DH)
        lax.fori_loop(2 * p, jnp.where(late, 2 * p, 2 * p + 2), local, 0)
        attended = jnp.concatenate(
            [num[2 * p + a] / (1.0 + den[2 * p + a]) for a in range(2)], axis=0
        )
        ss[0] = ss[0] + jnp.sum(attended * attended, axis=0, keepdims=True)
        gain = gain_mid_ref[:, pl.ds(pl.multiple_of(p * 2 * DH, 2 * DH), 2 * DH)]
        att[p] = (attended.T * gain.astype(jnp.float32)).astype(jnp.bfloat16)
        for k in range(1, nx):
            att_copy(k, p).start()
        return carry

    lax.fori_loop(0, pairs, second, 0)
    for k in range(1, nx):
        ss_copy(k).start()
    own = pl.ds(pl.multiple_of(hx * width, width), width)
    update = jnp.zeros((rows, width), jnp.float32)
    for p in range(pairs):
        update = update + dot(att[p], wo_ref[p * 2 * DH:(p + 1) * 2 * DH, own])
    for k in range(1, nx):
        wo_copy(k).wait()
        for p in range(pairs):
            att_copy(k, p).wait()
            update = update + dot(att_in[k, p], wo_in[k, p * 2 * DH:(p + 1) * 2 * DH, :])
    for k in range(1, nx):
        ss_copy(k).wait()
    squares = ss[0]
    for k in range(1, nx):
        squares = squares + ss[k]
    columns = jnp.broadcast_to(squares[:1], (128, rows)).T[:, :1]
    scale = lax.rsqrt(columns / full + EPSILON)
    out_ref[...] = (x_own[...].astype(jnp.float32) + update * scale).astype(jnp.bfloat16)

    @pl.when(me < n - 1)
    def _():
        for p in range(pairs):
            for i in range(PARTS):
                chain_copy(p, i).wait_send()


def shards(n, nx, tokens, w_qkv, w_out, gain_in, gain_mid):
    rows, width = tokens.shape
    features = w_qkv.shape[3]
    heads = features // DH
    pairs = heads // 2
    bf16, f32 = jnp.bfloat16, jnp.float32
    dma = pltpu.SemaphoreType.DMA
    return pl.pallas_call(
        functools.partial(kernel, n, nx),
        out_shape=jax.ShapeDtypeStruct((rows, width), bf16),
        in_specs=[pl.BlockSpec(memory_space=pl.ANY)] * 3
        + [pl.BlockSpec(memory_space=pltpu.VMEM)] * 2,
        out_specs=pl.BlockSpec(memory_space=pltpu.VMEM),
        scratch_shapes=[
            pltpu.VMEM((rows, width), bf16),
            pltpu.VMEM((3, nx * width, features), bf16),
            pltpu.VMEM((features, nx * width), bf16),
            pltpu.VMEM((nx, features, width), bf16),
            pltpu.VMEM((nx, rows, width), bf16),
            pltpu.VMEM((heads, DH, rows), bf16),
            pltpu.VMEM((heads, DH, rows), bf16),
            pltpu.VMEM((heads, DH, rows), bf16),
            pltpu.VMEM((pairs, rows, 2 * DH), bf16),
            pltpu.VMEM((2, FEATS, rows), bf16),
            pltpu.VMEM((2, rows // 128, 2 * DH, 128), f32),
            pltpu.VMEM((pairs, ROWS, 2 * DH), f32),
            pltpu.VMEM((pairs, PARTS, ROWS // PARTS, 2 * DH), bf16),
            pltpu.VMEM((pairs, PARTS, ROWS // PARTS, 2 * DH), bf16),
            pltpu.VMEM((heads, DH, rows), f32),
            pltpu.VMEM((heads, 1, rows), f32),
            pltpu.VMEM((pairs, rows, 2 * DH), bf16),
            pltpu.VMEM((nx, pairs, rows, 2 * DH), bf16),
            pltpu.VMEM((nx, 8, rows), f32),
            dma((3,)),
            dma((nx,)), dma((nx,)),
            dma((nx,)), dma((nx,)),
            dma((pairs, PARTS)), dma((pairs, PARTS)),
            dma((nx,)), dma((nx,)),
            dma((nx, pairs)), dma((nx, pairs)),
        ],
        compiler_params=pltpu.CompilerParams(
            collective_id=0, has_side_effects=True, vmem_limit_bytes=60 * 1024 * 1024
        ),
    )(tokens, w_qkv[0].transpose(1, 0, 2), w_out[0], gain_in, gain_mid)


def solution(mesh):
    placed = (
        P("seq", "head"),
        P(None, None, None, "head"),
        P(None, "head", None),
        P(),
        P(None, "head"),
    )
    return jax.shard_map(
        functools.partial(shards, mesh.shape["seq"], mesh.shape["head"]),
        mesh=mesh, in_specs=placed, out_specs=P("seq", "head"), check_vma=False,
    )
```

```python
import functools

import jax
import jax.numpy as jnp
from jax import lax
from jax.experimental import pallas as pl
from jax.experimental.pallas import tpu as pltpu
from jax.sharding import PartitionSpec as P

DH = 64
EPSILON = 1e-06
MESH = pl.DeviceIdType.MESH
TILE = 16
FEATS = DH * (DH // 2 + 1)
ROWS = FEATS + DH
GROUP = 4
PIECE = ROWS // 8


def dot(a, b, dims=((1,), (0,))):
    return lax.dot_general(a, b, (dims, ((), ())), preferred_element_type=jnp.float32)


def feature_tiles():
    tiles = []
    for r in range(TILE):
        for b in range(DH // TILE):
            for a in range(b + 1):
                if a < b or r <= TILE // 2:
                    tiles.append((a, b, r))
    return tiles


def kernel(
    n, nx, x_ref, w_hbm, wo_hbm, gain_in_ref, gain_mid_ref, out_ref,
    x_own, w_ref, wo_ref, wo_in, xbuf, q_t, k_t, v_t, v_pair, feat, twice, state, prefix,
    rs1_out, rs1_in, rs2_out, rs2_in, chain_out, chain_in, ag1_out, ag1_in, ag2_out,
    num, den, att, att_in, ss,
    load_sem, x_send, x_recv, wo_send, wo_recv, rs1_send, rs1_recv, rs2_send, rs2_recv,
    chain_send, chain_recv, ag1_send, ag1_recv, ag2_send, ag2_recv, ss_send, ss_recv,
    att_send, att_recv,
):
    me = lax.axis_index("seq")
    hx = lax.axis_index("head")
    rows, width = x_own.shape
    features = w_ref.shape[2]
    heads = features // DH
    pairs = heads // 2
    full = nx * width
    parts = 8 * pairs // GROUP
    planes = n // GROUP
    z, y, c = lax.div(me, GROUP), lax.rem(lax.div(me, 2), 2), lax.rem(me, 2)
    sibling, across_y = me + 1 - 2 * c, me + 2 - 4 * y
    above, below = lax.rem(me + GROUP, n), lax.rem(me + n - GROUP, n)

    def load(src, dst, i):
        return pltpu.make_async_copy(src, dst, load_sem.at[i])

    load(x_ref, x_own, 0).start()
    load(w_hbm, w_ref, 1).start()
    load(wo_hbm, wo_ref, 2).start()

    barrier = pltpu.get_barrier_semaphore()
    for neighbour in (sibling, across_y, above, below):
        pl.semaphore_signal(barrier, inc=1, device_id=(neighbour, hx), device_id_type=MESH)
    for k in range(1, nx):
        pl.semaphore_signal(
            barrier, inc=1, device_id=(me, lax.rem(hx + k, nx)), device_id_type=MESH
        )
    pl.semaphore_wait(barrier, 4 + nx - 1)

    def across(src, dst, send, recv, k):
        return pltpu.make_async_remote_copy(
            src_ref=src, dst_ref=dst, send_sem=send, recv_sem=recv,
            device_id=(me, lax.rem(hx + k, nx)), device_id_type=MESH,
        )

    def token_copy(k):
        return across(x_ref, xbuf.at[hx], x_send.at[k], x_recv.at[k], k)

    def wo_copy(k):
        at = pl.multiple_of(lax.rem(hx + k, nx) * width, width)
        return across(
            wo_ref.at[:, pl.ds(at, width)], wo_in.at[k], wo_send.at[k], wo_recv.at[k], k
        )

    def ss_copy(k):
        return across(ss.at[0], ss.at[k], ss_send.at[k], ss_recv.at[k], k)

    def att_copy(k, p):
        return across(att.at[p], att_in.at[k, p], att_send.at[k, p], att_recv.at[k, p], k)

    for k in range(1, nx):
        token_copy(k).start()

    num[...] = jnp.zeros_like(num)
    den[...] = jnp.zeros_like(den)
    ss[0] = jnp.zeros_like(ss[0])

    @pl.when(z == 0)
    def _():
        chain_in[...] = jnp.zeros_like(chain_in)

    load(x_ref, x_own, 0).wait()
    xbuf[hx] = x_own[...]
    load(w_hbm, w_ref, 1).wait()
    load(wo_hbm, wo_ref, 2).wait()
    for k in range(1, nx):
        token_copy(k).wait()
    for k in range(1, nx):
        wo_copy(k).start()

    total = jnp.zeros((rows, 1), jnp.float32)
    for j in range(nx):
        wide = xbuf[j].astype(jnp.float32)
        total = total + jnp.sum(wide * wide, axis=1, keepdims=True)
    inverse = lax.rsqrt(total / full + EPSILON)
    for j in range(nx):
        gain = gain_in_ref[:, j * width:(j + 1) * width].astype(jnp.float32)
        xbuf[j] = (xbuf[j].astype(jnp.float32) * inverse * gain).astype(jnp.bfloat16)

    def project(which):
        got = dot(xbuf[0], w_ref[which, :width, :])
        for j in range(1, nx):
            got = got + dot(xbuf[j], w_ref[which, j * width:(j + 1) * width, :])
        got = got.astype(jnp.bfloat16)
        (q_t, k_t, v_t)[which][...] = got.T.reshape(heads, DH, rows)
        if which == 2:
            for p in range(pairs):
                v_pair[p] = got[:, p * 2 * DH:(p + 1) * 2 * DH]

    low_lane = lax.broadcasted_iota(jnp.int32, (1, 2 * DH), 1) < DH
    tiles = feature_tiles()

    def expand(slot, u, edge, middle):
        wide = u.astype(jnp.float32)
        for j in range(rows // 128):
            lanes = slice(j * 128, (j + 1) * 128)
            for b in range(DH // TILE):
                tile = wide[b * TILE:(b + 1) * TILE, lanes]
                twice[slot, j, 2 * b * TILE:(2 * b + 1) * TILE, :] = tile
                twice[slot, j, (2 * b + 1) * TILE:(2 * b + 2) * TILE, :] = tile
        for j in range(rows // 128):
            lanes = slice(j * 128, (j + 1) * 128)
            rolled, held = None, None
            for at, (a, b, r) in enumerate(tiles):
                if held != (b, r):
                    low = 2 * b * TILE + r
                    rolled = twice[slot, j, low:low + TILE, :].astype(jnp.bfloat16)
                    held = (b, r)
                scaled = edge if a == b and r in (0, TILE // 2) else middle
                feat[slot, at * TILE:(at + 1) * TILE, lanes] = (
                    scaled[a * TILE:(a + 1) * TILE, lanes] * rolled
                )

    def make_state(p):
        both = jnp.concatenate([k_t[2 * p], k_t[2 * p + 1]], axis=0)
        values = v_pair[p]
        for a in range(2):
            u = k_t[2 * p + a]
            expand(a, u, u, u)
        for i in range(8):
            count = min(PIECE, FEATS - i * PIECE)
            at = slice(i * PIECE, i * PIECE + count)
            state[8 * p + i, :count, :] = jnp.where(
                low_lane, dot(feat[0, at, :], values), dot(feat[1, at, :], values)
            )
        state[8 * p + 7, PIECE - DH:, :] = jnp.where(
            low_lane, dot(k_t[2 * p], both, ((1,), (1,))), dot(k_t[2 * p + 1], both, ((1,), (1,)))
        )

    causal = lax.broadcasted_iota(jnp.int32, (rows, rows), 0) <= lax.broadcasted_iota(
        jnp.int32, (rows, rows), 1
    )

    def local(h, carry):
        scores = dot(k_t[h], q_t[h], ((0,), (0,)))
        weights = jnp.where(causal, scores * scores * (1.0 / DH), 0.0)
        den[h] = den[h] + jnp.sum(weights, axis=0, keepdims=True)
        num[h] = num[h] + dot(v_t[h], weights.astype(jnp.bfloat16))
        return carry

    def along(src, dst, send, recv, to):
        return pltpu.make_async_remote_copy(
            src_ref=src, dst_ref=dst, send_sem=send, recv_sem=recv,
            device_id=(to, hx), device_id_type=MESH,
        )

    def rs1_copy(line, i):
        return along(
            rs1_out.at[line, i], rs1_in.at[line, i], rs1_send.at[line, i], rs1_recv.at[line, i],
            sibling,
        )

    def rs2_copy(i):
        return along(rs2_out.at[i], rs2_in.at[i], rs2_send.at[i], rs2_recv.at[i], across_y)

    def chain_copy(i):
        return along(chain_out.at[i], chain_in.at[i], chain_send.at[i], chain_recv.at[i], above)

    def ag1_copy(i):
        return along(ag1_out.at[i], ag1_in.at[i], ag1_send.at[i], ag1_recv.at[i], across_y)

    def ag2_copy(line, i):
        return along(
            ag2_out.at[line, i], prefix.at[(2 * line + c) * parts + i], ag2_send.at[line, i],
            ag2_recv.at[line, i], sibling,
        )

    def wide(value):
        return value.astype(jnp.float32)

    def narrow(value):
        return value.astype(jnp.bfloat16)

    is_second_core, is_second_line = c.astype(jnp.float32), y.astype(jnp.float32)

    def make_unit(unit):
        if pairs >= GROUP:
            for j in range(pairs // GROUP):
                make_state(unit * (pairs // GROUP) + j)

    def give(line, unit):
        make_unit(unit)
        for i in range(parts):
            rs1_out[line, i] = narrow(state[unit * parts + i])
            rs1_copy(line, i).start()

    def settle(line, i, chip_prefix):
        at = (2 * line + c) * parts + i
        prefix[at] = narrow(chip_prefix + is_second_core * wide(rs1_in[line, i]))
        ag2_out[line, i] = narrow(chip_prefix + (1.0 - is_second_core) * state[at])
        ag2_copy(line, i).start()

    def own_part(i):
        rs1_copy(y, i).wait_recv()
        rs2_copy(i).wait_recv()

        @pl.when(z > 0)
        def _():
            chain_copy(i).wait_recv()

        mine = state[(2 * y + c) * parts + i] + wide(rs1_in[y, i])
        other = wide(rs2_in[i])
        before = wide(chain_in[i])

        @pl.when(z < planes - 1)
        def _():
            chain_out[i] = narrow(before + mine + other)
            chain_copy(i).start()

        ag1_out[i] = narrow(before + (1.0 - is_second_line) * mine)
        ag1_copy(i).start()
        settle(y, i, before + is_second_line * other)

    late = z >= planes // 2

    project(1)
    project(2)
    if pairs < GROUP:
        for p in range(pairs):
            make_state(p)
    far = 1 - y
    give(far, 2 * far + 1 - c)
    make_unit(2 * far + c)
    for i in range(parts):
        rs1_copy(far, i).wait_recv()
        rs2_out[i] = narrow(state[(2 * far + c) * parts + i] + wide(rs1_in[far, i]))
        rs2_copy(i).start()
    give(y, 2 * y + 1 - c)
    make_unit(2 * y + c)
    project(0)
    lax.fori_loop(0, jnp.where(late, heads, 0), local, 0)
    for i in range(parts):
        own_part(i)

    def far_parts():
        for i in range(parts):
            ag1_copy(i).wait_recv()
            settle(far, i, wide(ag1_in[i]))

    def query(p):
        whole = prefix[pl.ds(8 * p, 8)].reshape(ROWS, 2 * DH).T
        for a in range(2):
            h = 2 * p + a
            u = q_t[h]
            expand(a, u, u * (1.0 / DH), u * (2.0 / DH))
            mine = whole[a * DH:(a + 1) * DH, :]
            num[h] = num[h] + dot(mine[:, :FEATS], feat[a])
            gram = dot(mine[:, FEATS:], u)
            den[h] = den[h] + jnp.sum(
                gram * u.astype(jnp.float32), axis=0, keepdims=True
            ) * (1.0 / DH)
        lax.fori_loop(2 * p, jnp.where(late, 2 * p, 2 * p + 2), local, 0)
        attended = jnp.concatenate(
            [num[2 * p + a] / (1.0 + den[2 * p + a]) for a in range(2)], axis=0
        )
        ss[0] = ss[0] + jnp.sum(attended * attended, axis=0, keepdims=True)
        gain = gain_mid_ref[:, pl.ds(pl.multiple_of(p * 2 * DH, 2 * DH), 2 * DH)]
        att[p] = (attended.T * gain.astype(jnp.float32)).astype(jnp.bfloat16)
        for k in range(1, nx):
            att_copy(k, p).start()

    if pairs >= GROUP:

        def turn(step, carry):
            line = jnp.where(step < 2, y, far)
            core = jnp.where(lax.rem(step, 2) == 0, c, 1 - c)

            @pl.when(step == 1)
            def _():
                far_parts()

            @pl.when(core != c)
            def _():
                for i in range(parts):
                    ag2_copy(line, i).wait_recv()

            for j in range(pairs // GROUP):
                query((2 * line + core) * (pairs // GROUP) + j)
            return carry

        lax.fori_loop(0, GROUP, turn, 0)
    else:
        far_parts()
        for i in range(parts):
            for line in range(2):
                ag2_copy(line, i).wait_recv()
        for p in range(pairs):
            query(p)
    for k in range(1, nx):
        ss_copy(k).start()
    own = pl.ds(pl.multiple_of(hx * width, width), width)
    update = jnp.zeros((rows, width), jnp.float32)
    for p in range(pairs):
        update = update + dot(att[p], wo_ref[p * 2 * DH:(p + 1) * 2 * DH, own])
    for k in range(1, nx):
        wo_copy(k).wait()
        for p in range(pairs):
            att_copy(k, p).wait()
            update = update + dot(att_in[k, p], wo_in[k, p * 2 * DH:(p + 1) * 2 * DH, :])
    for k in range(1, nx):
        ss_copy(k).wait()
    squares = ss[0]
    for k in range(1, nx):
        squares = squares + ss[k]
    columns = jnp.broadcast_to(squares[:1], (128, rows)).T[:, :1]
    scale = lax.rsqrt(columns / full + EPSILON)
    out_ref[...] = (x_own[...].astype(jnp.float32) + update * scale).astype(jnp.bfloat16)

    for i in range(parts):
        for line in range(2):
            rs1_copy(line, i).wait_send()
            ag2_copy(line, i).wait_send()
        rs2_copy(i).wait_send()
        ag1_copy(i).wait_send()

    @pl.when(z < planes - 1)
    def _():
        for i in range(parts):
            chain_copy(i).wait_send()


def shards(n, nx, tokens, w_qkv, w_out, gain_in, gain_mid):
    rows, width = tokens.shape
    features = w_qkv.shape[3]
    heads = features // DH
    pairs = heads // 2
    parts = 8 * pairs // GROUP
    bf16, f32 = jnp.bfloat16, jnp.float32
    dma = pltpu.SemaphoreType.DMA
    return pl.pallas_call(
        functools.partial(kernel, n, nx),
        out_shape=jax.ShapeDtypeStruct((rows, width), bf16),
        in_specs=[pl.BlockSpec(memory_space=pl.ANY)] * 3
        + [pl.BlockSpec(memory_space=pltpu.VMEM)] * 2,
        out_specs=pl.BlockSpec(memory_space=pltpu.VMEM),
        scratch_shapes=[
            pltpu.VMEM((rows, width), bf16),
            pltpu.VMEM((3, nx * width, features), bf16),
            pltpu.VMEM((features, nx * width), bf16),
            pltpu.VMEM((nx, features, width), bf16),
            pltpu.VMEM((nx, rows, width), bf16),
            pltpu.VMEM((heads, DH, rows), bf16),
            pltpu.VMEM((heads, DH, rows), bf16),
            pltpu.VMEM((heads, DH, rows), bf16),
            pltpu.VMEM((pairs, rows, 2 * DH), bf16),
            pltpu.VMEM((2, FEATS, rows), bf16),
            pltpu.VMEM((2, rows // 128, 2 * DH, 128), f32),
            pltpu.VMEM((8 * pairs, PIECE, 2 * DH), f32),
            pltpu.VMEM((8 * pairs, PIECE, 2 * DH), bf16),
            pltpu.VMEM((2, parts, PIECE, 2 * DH), bf16),
            pltpu.VMEM((2, parts, PIECE, 2 * DH), bf16),
            pltpu.VMEM((parts, PIECE, 2 * DH), bf16),
            pltpu.VMEM((parts, PIECE, 2 * DH), bf16),
            pltpu.VMEM((parts, PIECE, 2 * DH), bf16),
            pltpu.VMEM((parts, PIECE, 2 * DH), bf16),
            pltpu.VMEM((parts, PIECE, 2 * DH), bf16),
            pltpu.VMEM((parts, PIECE, 2 * DH), bf16),
            pltpu.VMEM((2, parts, PIECE, 2 * DH), bf16),
            pltpu.VMEM((heads, DH, rows), f32),
            pltpu.VMEM((heads, 1, rows), f32),
            pltpu.VMEM((pairs, rows, 2 * DH), bf16),
            pltpu.VMEM((nx, pairs, rows, 2 * DH), bf16),
            pltpu.VMEM((nx, 8, rows), f32),
            dma((3,)),
            dma((nx,)), dma((nx,)),
            dma((nx,)), dma((nx,)),
            dma((2, parts)), dma((2, parts)),
            dma((parts,)), dma((parts,)),
            dma((parts,)), dma((parts,)),
            dma((parts,)), dma((parts,)),
            dma((2, parts)), dma((2, parts)),
            dma((nx,)), dma((nx,)),
            dma((nx, pairs)), dma((nx, pairs)),
        ],
        compiler_params=pltpu.CompilerParams(
            collective_id=0, has_side_effects=True, vmem_limit_bytes=60 * 1024 * 1024
        ),
    )(tokens, w_qkv[0].transpose(1, 0, 2), w_out[0], gain_in, gain_mid)


def solution(mesh):
    placed = (
        P("seq", "head"),
        P(None, None, None, "head"),
        P(None, "head", None),
        P(),
        P(None, "head"),
    )
    return jax.shard_map(
        functools.partial(shards, mesh.shape["seq"], mesh.shape["head"]),
        mesh=mesh, in_specs=placed, out_specs=P("seq", "head"), check_vma=False,
    )
```

```python
import functools

import jax
import jax.numpy as jnp
from jax import lax
from jax.experimental import pallas as pl
from jax.experimental.pallas import tpu as pltpu
from jax.sharding import PartitionSpec as P

DH = 64
EPSILON = 1e-06
MESH = pl.DeviceIdType.MESH
TILE = 16
FEATS = DH * (DH // 2 + 1)
ROWS = FEATS + DH
GROUP = 4
CHUNKS = 4
PIECE = ROWS // 8


def dot(a, b, dims=((1,), (0,))):
    return lax.dot_general(a, b, (dims, ((), ())), preferred_element_type=jnp.float32)


def feature_tiles():
    tiles = []
    for r in range(TILE):
        for b in range(DH // TILE):
            for a in range(b + 1):
                if a < b or r <= TILE // 2:
                    tiles.append((a, b, r))
    return tiles


def kernel(
    n, nx, x_ref, w_hbm, wo_hbm, gain_in_ref, gain_mid_ref, out_ref,
    x_own, w_ref, wo_ref, wo_in, xbuf, q_t, k_t, v_t, v_pair, feat, twice, state, prefix,
    rs1_out, rs1_in, rs2_out, rs2_in, chain_out, chain_in, ag1_out, ag1_in, ag2_out,
    num, den, att, att_in, ss,
    load_sem, x_send, x_recv, wo_send, wo_recv, rs1_send, rs1_recv, rs2_send, rs2_recv,
    chain_send, chain_recv, ag1_send, ag1_recv, ag2_send, ag2_recv, ss_send, ss_recv,
    att_send, att_recv,
):
    me = lax.axis_index("seq")
    hx = lax.axis_index("head")
    rows, width = x_own.shape
    features = w_ref.shape[2]
    heads = features // DH
    pairs = heads // 2
    full = nx * width
    parts = 8 * pairs // GROUP
    planes = n // GROUP
    z, y, c = lax.div(me, GROUP), lax.rem(lax.div(me, 2), 2), lax.rem(me, 2)
    sibling, across_y = me + 1 - 2 * c, me + 2 - 4 * y
    above, below = lax.rem(me + GROUP, n), lax.rem(me + n - GROUP, n)

    def load(src, dst, i):
        return pltpu.make_async_copy(src, dst, load_sem.at[i])

    load(x_ref, x_own, 0).start()
    load(w_hbm, w_ref, 1).start()
    load(wo_hbm, wo_ref, 2).start()

    barrier = pltpu.get_barrier_semaphore()
    for neighbour in (sibling, across_y, above, below):
        pl.semaphore_signal(barrier, inc=1, device_id=(neighbour, hx), device_id_type=MESH)
    for k in range(1, nx):
        pl.semaphore_signal(
            barrier, inc=1, device_id=(me, lax.rem(hx + k, nx)), device_id_type=MESH
        )
    pl.semaphore_wait(barrier, 4 + nx - 1)

    def across(src, dst, send, recv, k):
        return pltpu.make_async_remote_copy(
            src_ref=src, dst_ref=dst, send_sem=send, recv_sem=recv,
            device_id=(me, lax.rem(hx + k, nx)), device_id_type=MESH,
        )

    chunk = rows // CHUNKS

    def token_copy(k, j):
        at = pl.ds(j * chunk, chunk)
        return across(x_ref.at[at], xbuf.at[hx, at], x_send.at[k, j], x_recv.at[k, j], k)

    def wo_copy(k):
        at = pl.multiple_of(lax.rem(hx + k, nx) * width, width)
        return across(
            wo_ref.at[:, pl.ds(at, width)], wo_in.at[k], wo_send.at[k], wo_recv.at[k], k
        )

    def ss_copy(k):
        return across(ss.at[0], ss.at[k], ss_send.at[k], ss_recv.at[k], k)

    def att_copy(k, p):
        return across(att.at[p], att_in.at[k, p], att_send.at[k, p], att_recv.at[k, p], k)

    for j in range(CHUNKS):
        for k in range(1, nx):
            token_copy(k, j).start()

    num[...] = jnp.zeros_like(num)
    den[...] = jnp.zeros_like(den)
    ss[0] = jnp.zeros_like(ss[0])

    @pl.when(z == 0)
    def _():
        chain_in[...] = jnp.zeros_like(chain_in)

    load(x_ref, x_own, 0).wait()
    xbuf[hx] = x_own[...]
    load(w_hbm, w_ref, 1).wait()
    load(wo_hbm, wo_ref, 2).wait()
    for j in range(CHUNKS):
        at = slice(j * chunk, (j + 1) * chunk)
        for k in range(1, nx):
            token_copy(k, j).wait()
        blocks = [xbuf[i, at, :].astype(jnp.float32) for i in range(nx)]
        total = sum(jnp.sum(block * block, axis=1, keepdims=True) for block in blocks)
        inverse = lax.rsqrt(total / full + EPSILON)
        normed = [
            (block * inverse * gain_in_ref[:, i * width:(i + 1) * width].astype(jnp.float32)).astype(
                jnp.bfloat16
            )
            for i, block in enumerate(blocks)
        ]
        for which in range(3):
            got = dot(normed[0], w_ref[which, :width, :])
            for i in range(1, nx):
                got = got + dot(normed[i], w_ref[which, i * width:(i + 1) * width, :])
            got = got.astype(jnp.bfloat16)
            (q_t, k_t, v_t)[which][:, :, at] = got.T.reshape(heads, DH, chunk)
            if which == 2:
                for p in range(pairs):
                    v_pair[p, at, :] = got[:, p * 2 * DH:(p + 1) * 2 * DH]
    for k in range(1, nx):
        wo_copy(k).start()

    low_lane = lax.broadcasted_iota(jnp.int32, (1, 2 * DH), 1) < DH
    tiles = feature_tiles()

    def expand(slot, spare, u, edge, middle):
        wide = u.astype(jnp.float32)
        for j in range(rows // 128):
            lanes = slice(j * 128, (j + 1) * 128)
            for b in range(DH // TILE):
                tile = wide[b * TILE:(b + 1) * TILE, lanes]
                twice[spare, j, 2 * b * TILE:(2 * b + 1) * TILE, :] = tile
                twice[spare, j, (2 * b + 1) * TILE:(2 * b + 2) * TILE, :] = tile
        for j in range(rows // 128):
            lanes = slice(j * 128, (j + 1) * 128)
            rolled, held = None, None
            for at, (a, b, r) in enumerate(tiles):
                if held != (b, r):
                    low = 2 * b * TILE + r
                    rolled = twice[spare, j, low:low + TILE, :].astype(jnp.bfloat16)
                    held = (b, r)
                scaled = edge if a == b and r in (0, TILE // 2) else middle
                feat[slot, at * TILE:(at + 1) * TILE, lanes] = (
                    scaled[a * TILE:(a + 1) * TILE, lanes] * rolled
                )

    def make_state(p):
        both = jnp.concatenate([k_t[2 * p], k_t[2 * p + 1]], axis=0)
        values = v_pair[p]
        for a in range(2):
            u = k_t[2 * p + a]
            expand(a, a, u, u, u)
        for i in range(8):
            count = min(PIECE, FEATS - i * PIECE)
            at = slice(i * PIECE, i * PIECE + count)
            state[8 * p + i, :count, :] = jnp.where(
                low_lane, dot(feat[0, at, :], values), dot(feat[1, at, :], values)
            )
        state[8 * p + 7, PIECE - DH:, :] = jnp.where(
            low_lane, dot(k_t[2 * p], both, ((1,), (1,))), dot(k_t[2 * p + 1], both, ((1,), (1,)))
        )

    half = rows // 2
    causal = lax.broadcasted_iota(jnp.int32, (half, half), 0) <= lax.broadcasted_iota(
        jnp.int32, (half, half), 1
    )

    def local(h, carry):
        def weigh(s_at, t_at, masked):
            scores = dot(k_t[h, :, s_at], q_t[h, :, t_at], ((0,), (0,)))
            weights = scores * scores * (1.0 / DH)
            if masked:
                weights = jnp.where(causal, weights, 0.0)
            total = jnp.sum(weights, axis=0, keepdims=True)
            return total, dot(v_t[h, :, s_at], weights.astype(jnp.bfloat16))

        low, high = slice(0, half), slice(half, rows)
        den_a, num_a = weigh(low, low, True)
        den_b, num_b = weigh(low, high, False)
        den_c, num_c = weigh(high, high, True)
        den[h, :, low] = den[h, :, low] + den_a
        den[h, :, high] = den[h, :, high] + (den_b + den_c)
        num[h, :, low] = num[h, :, low] + num_a
        num[h, :, high] = num[h, :, high] + (num_b + num_c)
        return carry

    def along(src, dst, send, recv, to):
        return pltpu.make_async_remote_copy(
            src_ref=src, dst_ref=dst, send_sem=send, recv_sem=recv,
            device_id=(to, hx), device_id_type=MESH,
        )

    def rs1_copy(line, i):
        return along(
            rs1_out.at[line, i], rs1_in.at[line, i], rs1_send.at[line, i], rs1_recv.at[line, i],
            sibling,
        )

    def rs2_copy(i):
        return along(rs2_out.at[i], rs2_in.at[i], rs2_send.at[i], rs2_recv.at[i], across_y)

    def chain_copy(i):
        return along(chain_out.at[i], chain_in.at[i], chain_send.at[i], chain_recv.at[i], above)

    def ag1_copy(i):
        return along(ag1_out.at[i], ag1_in.at[i], ag1_send.at[i], ag1_recv.at[i], across_y)

    def ag2_copy(line, i):
        return along(
            ag2_out.at[line, i], prefix.at[(2 * line + c) * parts + i], ag2_send.at[line, i],
            ag2_recv.at[line, i], sibling,
        )

    def wide(value):
        return value.astype(jnp.float32)

    def narrow(value):
        return value.astype(jnp.bfloat16)

    is_second_core, is_second_line = c.astype(jnp.float32), y.astype(jnp.float32)

    def make_unit(unit):
        if pairs >= GROUP:
            for j in range(pairs // GROUP):
                make_state(unit * (pairs // GROUP) + j)

    def give(line, unit):
        make_unit(unit)
        for i in range(parts):
            rs1_out[line, i] = narrow(state[unit * parts + i])
            rs1_copy(line, i).start()

    def settle(line, i, chip_prefix):
        at = (2 * line + c) * parts + i
        prefix[at] = narrow(chip_prefix + is_second_core * wide(rs1_in[line, i]))
        ag2_out[line, i] = narrow(chip_prefix + (1.0 - is_second_core) * state[at])
        ag2_copy(line, i).start()

    def own_part(i):
        rs1_copy(y, i).wait_recv()
        rs2_copy(i).wait_recv()

        @pl.when(z > 0)
        def _():
            chain_copy(i).wait_recv()

        mine = state[(2 * y + c) * parts + i] + wide(rs1_in[y, i])
        other = wide(rs2_in[i])
        before = wide(chain_in[i])

        @pl.when(z < planes - 1)
        def _():
            chain_out[i] = narrow(before + mine + other)
            chain_copy(i).start()

        ag1_out[i] = narrow(before + (1.0 - is_second_line) * mine)
        ag1_copy(i).start()
        settle(y, i, before + is_second_line * other)

    late = z >= planes // 2

    if pairs < GROUP:
        for p in range(pairs):
            make_state(p)
    far = 1 - y
    give(far, 2 * far + 1 - c)
    make_unit(2 * far + c)
    for i in range(parts):
        rs1_copy(far, i).wait_recv()
        rs2_out[i] = narrow(state[(2 * far + c) * parts + i] + wide(rs1_in[far, i]))
        rs2_copy(i).start()
    give(y, 2 * y + 1 - c)
    make_unit(2 * y + c)
    per = pairs // GROUP

    def fill(slot, spare, h):
        u = q_t[h]
        expand(slot, spare, u, u * (1.0 / DH), u * (2.0 / DH))

    def fill_far(core, carry):
        for j in range(per):
            for a in range(2):
                fill(2 + 2 * (per * core + j) + a, a, 2 * (per * (2 * far + core) + j) + a)
        return carry

    last = z == planes - 1
    lax.fori_loop(0, jnp.where(late, heads, 0), local, 0)
    lax.fori_loop(0, jnp.where(last, 2, 0), fill_far, 0)
    for i in range(parts):
        own_part(i)
    lax.fori_loop(0, jnp.where(late, 0, heads), local, 0)

    def far_parts():
        for i in range(parts):
            ag1_copy(i).wait_recv()
            settle(far, i, wide(ag1_in[i]))

    def query(p, slot, filled):
        whole = prefix[pl.ds(8 * p, 8)].reshape(ROWS, 2 * DH).T
        for a in range(2):
            h = 2 * p + a
            u = q_t[h]
            if not filled:
                fill(slot + a, a, h)
            mine = whole[a * DH:(a + 1) * DH, :]
            num[h] = num[h] + dot(mine[:, :FEATS], feat[slot + a])
            gram = dot(mine[:, FEATS:], u)
            den[h] = den[h] + jnp.sum(
                gram * u.astype(jnp.float32), axis=0, keepdims=True
            ) * (1.0 / DH)
        attended = jnp.concatenate(
            [num[2 * p + a] / (1.0 + den[2 * p + a]) for a in range(2)], axis=0
        )
        ss[0] = ss[0] + jnp.sum(attended * attended, axis=0, keepdims=True)
        gain = gain_mid_ref[:, pl.ds(pl.multiple_of(p * 2 * DH, 2 * DH), 2 * DH)]
        att[p] = (attended.T * gain.astype(jnp.float32)).astype(jnp.bfloat16)
        for k in range(1, nx):
            att_copy(k, p).start()

    if pairs >= GROUP:

        def near(step, carry):
            core = jnp.where(step == 0, c, 1 - c)

            @pl.when(step == 1)
            def _():
                for i in range(parts):
                    ag2_copy(y, i).wait_recv()

            for j in range(per):
                query((2 * y + core) * per + j, 0, False)
            return carry

        def distant(step, carry):
            core = jnp.where(step == 0, c, 1 - c)

            @pl.when(step == 1)
            def _():
                for i in range(parts):
                    ag2_copy(far, i).wait_recv()

            for j in range(per):
                query((2 * far + core) * per + j, 2 + 2 * (per * core + j), True)
            return carry

        lax.fori_loop(0, 2, near, 0)
        lax.fori_loop(0, jnp.where(last, 0, 2), fill_far, 0)
        far_parts()
        lax.fori_loop(0, 2, distant, 0)
    else:
        far_parts()
        for i in range(parts):
            for line in range(2):
                ag2_copy(line, i).wait_recv()
        for p in range(pairs):
            query(p, 0, False)
    for k in range(1, nx):
        ss_copy(k).start()
    own = pl.ds(pl.multiple_of(hx * width, width), width)
    update = jnp.zeros((rows, width), jnp.float32)
    for p in range(pairs):
        update = update + dot(att[p], wo_ref[p * 2 * DH:(p + 1) * 2 * DH, own])
    for k in range(1, nx):
        wo_copy(k).wait()
        for p in range(pairs):
            att_copy(k, p).wait()
            update = update + dot(att_in[k, p], wo_in[k, p * 2 * DH:(p + 1) * 2 * DH, :])
    for k in range(1, nx):
        ss_copy(k).wait()
    squares = ss[0]
    for k in range(1, nx):
        squares = squares + ss[k]
    columns = jnp.broadcast_to(squares[:1], (128, rows)).T[:, :1]
    scale = lax.rsqrt(columns / full + EPSILON)
    out_ref[...] = (x_own[...].astype(jnp.float32) + update * scale).astype(jnp.bfloat16)

    for i in range(parts):
        for line in range(2):
            rs1_copy(line, i).wait_send()
            ag2_copy(line, i).wait_send()
        rs2_copy(i).wait_send()
        ag1_copy(i).wait_send()

    @pl.when(z < planes - 1)
    def _():
        for i in range(parts):
            chain_copy(i).wait_send()


def shards(n, nx, tokens, w_qkv, w_out, gain_in, gain_mid):
    rows, width = tokens.shape
    features = w_qkv.shape[3]
    heads = features // DH
    pairs = heads // 2
    parts = 8 * pairs // GROUP
    bf16, f32 = jnp.bfloat16, jnp.float32
    dma = pltpu.SemaphoreType.DMA
    return pl.pallas_call(
        functools.partial(kernel, n, nx),
        out_shape=jax.ShapeDtypeStruct((rows, width), bf16),
        in_specs=[pl.BlockSpec(memory_space=pl.ANY)] * 3
        + [pl.BlockSpec(memory_space=pltpu.VMEM)] * 2,
        out_specs=pl.BlockSpec(memory_space=pltpu.VMEM),
        scratch_shapes=[
            pltpu.VMEM((rows, width), bf16),
            pltpu.VMEM((3, nx * width, features), bf16),
            pltpu.VMEM((features, nx * width), bf16),
            pltpu.VMEM((nx, features, width), bf16),
            pltpu.VMEM((nx, rows, width), bf16),
            pltpu.VMEM((heads, DH, rows), bf16),
            pltpu.VMEM((heads, DH, rows), bf16),
            pltpu.VMEM((heads, DH, rows), bf16),
            pltpu.VMEM((pairs, rows, 2 * DH), bf16),
            pltpu.VMEM((2 + 4 * (pairs // GROUP), FEATS, rows), bf16),
            pltpu.VMEM((2, rows // 128, 2 * DH, 128), f32),
            pltpu.VMEM((8 * pairs, PIECE, 2 * DH), f32),
            pltpu.VMEM((8 * pairs, PIECE, 2 * DH), bf16),
            pltpu.VMEM((2, parts, PIECE, 2 * DH), bf16),
            pltpu.VMEM((2, parts, PIECE, 2 * DH), bf16),
            pltpu.VMEM((parts, PIECE, 2 * DH), bf16),
            pltpu.VMEM((parts, PIECE, 2 * DH), bf16),
            pltpu.VMEM((parts, PIECE, 2 * DH), bf16),
            pltpu.VMEM((parts, PIECE, 2 * DH), bf16),
            pltpu.VMEM((parts, PIECE, 2 * DH), bf16),
            pltpu.VMEM((parts, PIECE, 2 * DH), bf16),
            pltpu.VMEM((2, parts, PIECE, 2 * DH), bf16),
            pltpu.VMEM((heads, DH, rows), f32),
            pltpu.VMEM((heads, 1, rows), f32),
            pltpu.VMEM((pairs, rows, 2 * DH), bf16),
            pltpu.VMEM((nx, pairs, rows, 2 * DH), bf16),
            pltpu.VMEM((nx, 8, rows), f32),
            dma((3,)),
            dma((nx, CHUNKS)), dma((nx, CHUNKS)),
            dma((nx,)), dma((nx,)),
            dma((2, parts)), dma((2, parts)),
            dma((parts,)), dma((parts,)),
            dma((parts,)), dma((parts,)),
            dma((parts,)), dma((parts,)),
            dma((2, parts)), dma((2, parts)),
            dma((nx,)), dma((nx,)),
            dma((nx, pairs)), dma((nx, pairs)),
        ],
        compiler_params=pltpu.CompilerParams(
            collective_id=0, has_side_effects=True, vmem_limit_bytes=60 * 1024 * 1024
        ),
    )(tokens, w_qkv[0].transpose(1, 0, 2), w_out[0], gain_in, gain_mid)


def solution(mesh):
    placed = (
        P("seq", "head"),
        P(None, None, None, "head"),
        P(None, "head", None),
        P(),
        P(None, "head"),
    )
    return jax.shard_map(
        functools.partial(shards, mesh.shape["seq"], mesh.shape["head"]),
        mesh=mesh, in_specs=placed, out_specs=P("seq", "head"), check_vma=False,
    )
```

```python
import functools

import jax
import jax.numpy as jnp
from jax import lax
from jax.experimental import pallas as pl
from jax.experimental.pallas import tpu as pltpu
from jax.sharding import PartitionSpec as P

DH = 64
EPSILON = 1e-06
MESH = pl.DeviceIdType.MESH
TILE = 16
FEATS = DH * (DH // 2 + 1)
ROWS = FEATS + DH
GROUP = 4
CHUNKS = 4
PIECE = ROWS // 8


def dot(a, b, dims=((1,), (0,))):
    return lax.dot_general(a, b, (dims, ((), ())), preferred_element_type=jnp.float32)


def feature_tiles():
    tiles = []
    for r in range(TILE):
        for b in range(DH // TILE):
            for a in range(b + 1):
                if a < b or r <= TILE // 2:
                    tiles.append((a, b, r))
    return tiles


def kernel(
    n, nx, x_ref, w_hbm, wo_hbm, gain_in_ref, gain_mid_ref, out_ref,
    x_own, w_ref, wo_ref, wo_in, xbuf, q_t, k_t, v_t, v_pair, feat, twice, state, prefix,
    rs1_out, rs1_in, rs2_out, rs2_in, chain_out, chain_in, ag1_out, ag1_in, ag2_out,
    num, den, att, att_in, ss,
    load_sem, x_send, x_recv, wo_send, wo_recv, rs1_send, rs1_recv, rs2_send, rs2_recv,
    chain_send, chain_recv, ag1_send, ag1_recv, ag2_send, ag2_recv, ss_send, ss_recv,
    att_send, att_recv,
):
    me = lax.axis_index("seq")
    hx = lax.axis_index("head")
    rows, width = x_own.shape
    features = w_ref.shape[2]
    heads = features // DH
    pairs = heads // 2
    full = nx * width
    parts = 8 * pairs // GROUP
    planes = n // GROUP
    z, y, c = lax.div(me, GROUP), lax.rem(lax.div(me, 2), 2), lax.rem(me, 2)
    sibling, across_y = me + 1 - 2 * c, me + 2 - 4 * y
    above, below = lax.rem(me + GROUP, n), lax.rem(me + n - GROUP, n)

    def load(src, dst, i):
        return pltpu.make_async_copy(src, dst, load_sem.at[i])

    load(x_ref, x_own, 0).start()
    load(w_hbm, w_ref, 1).start()
    load(wo_hbm, wo_ref, 2).start()

    barrier = pltpu.get_barrier_semaphore()
    for neighbour in (sibling, across_y, above, below):
        pl.semaphore_signal(barrier, inc=1, device_id=(neighbour, hx), device_id_type=MESH)
    for k in range(1, nx):
        pl.semaphore_signal(
            barrier, inc=1, device_id=(me, lax.rem(hx + k, nx)), device_id_type=MESH
        )
    pl.semaphore_wait(barrier, 4 + nx - 1)

    def across(src, dst, send, recv, k):
        return pltpu.make_async_remote_copy(
            src_ref=src, dst_ref=dst, send_sem=send, recv_sem=recv,
            device_id=(me, lax.rem(hx + k, nx)), device_id_type=MESH,
        )

    chunk = rows // CHUNKS

    def token_copy(k, j):
        at = pl.ds(j * chunk, chunk)
        return across(x_ref.at[at], xbuf.at[hx, at], x_send.at[k, j], x_recv.at[k, j], k)

    def wo_copy(k):
        at = pl.multiple_of(lax.rem(hx + k, nx) * width, width)
        return across(
            wo_ref.at[:, pl.ds(at, width)], wo_in.at[k], wo_send.at[k], wo_recv.at[k], k
        )

    def ss_copy(k):
        return across(ss.at[0], ss.at[k], ss_send.at[k], ss_recv.at[k], k)

    def att_copy(k, p):
        return across(att.at[p], att_in.at[k, p], att_send.at[k, p], att_recv.at[k, p], k)

    for j in range(CHUNKS):
        for k in range(1, nx):
            token_copy(k, j).start()

    num[...] = jnp.zeros_like(num)
    den[...] = jnp.zeros_like(den)
    ss[0] = jnp.zeros_like(ss[0])

    @pl.when(z == 0)
    def _():
        chain_in[...] = jnp.zeros_like(chain_in)

    load(x_ref, x_own, 0).wait()
    xbuf[hx] = x_own[...]
    load(w_hbm, w_ref, 1).wait()
    load(wo_hbm, wo_ref, 2).wait()
    for j in range(CHUNKS):
        at = slice(j * chunk, (j + 1) * chunk)
        for k in range(1, nx):
            token_copy(k, j).wait()
        blocks = [xbuf[i, at, :].astype(jnp.float32) for i in range(nx)]
        total = sum(jnp.sum(block * block, axis=1, keepdims=True) for block in blocks)
        inverse = lax.rsqrt(total / full + EPSILON)
        normed = [
            (block * inverse * gain_in_ref[:, i * width:(i + 1) * width].astype(jnp.float32)).astype(
                jnp.bfloat16
            )
            for i, block in enumerate(blocks)
        ]
        for which in range(3):
            got = dot(normed[0], w_ref[which, :width, :])
            for i in range(1, nx):
                got = got + dot(normed[i], w_ref[which, i * width:(i + 1) * width, :])
            got = got.astype(jnp.bfloat16)
            (q_t, k_t, v_t)[which][:, :, at] = got.T.reshape(heads, DH, chunk)
            if which == 2:
                for p in range(pairs):
                    v_pair[p, at, :] = got[:, p * 2 * DH:(p + 1) * 2 * DH]
    for k in range(1, nx):
        wo_copy(k).start()

    low_lane = lax.broadcasted_iota(jnp.int32, (1, 2 * DH), 1) < DH
    tiles = feature_tiles()

    def expand(slot, spare, u, edge, middle):
        wide = u.astype(jnp.float32)
        for j in range(rows // 128):
            lanes = slice(j * 128, (j + 1) * 128)
            for b in range(DH // TILE):
                tile = wide[b * TILE:(b + 1) * TILE, lanes]
                twice[spare, j, 2 * b * TILE:(2 * b + 1) * TILE, :] = tile
                twice[spare, j, (2 * b + 1) * TILE:(2 * b + 2) * TILE, :] = tile
        for j in range(rows // 128):
            lanes = slice(j * 128, (j + 1) * 128)
            rolled, held = None, None
            for at, (a, b, r) in enumerate(tiles):
                if held != (b, r):
                    low = 2 * b * TILE + r
                    rolled = twice[spare, j, low:low + TILE, :].astype(jnp.bfloat16)
                    held = (b, r)
                scaled = edge if a == b and r in (0, TILE // 2) else middle
                feat[slot, at * TILE:(at + 1) * TILE, lanes] = (
                    scaled[a * TILE:(a + 1) * TILE, lanes] * rolled
                )

    def make_state(p):
        both = jnp.concatenate([k_t[2 * p], k_t[2 * p + 1]], axis=0)
        values = v_pair[p]
        for a in range(2):
            u = k_t[2 * p + a]
            expand(a, a, u, u, u)
        for i in range(8):
            count = min(PIECE, FEATS - i * PIECE)
            at = slice(i * PIECE, i * PIECE + count)
            state[8 * p + i, :count, :] = jnp.where(
                low_lane, dot(feat[0, at, :], values), dot(feat[1, at, :], values)
            )
        state[8 * p + 7, PIECE - DH:, :] = jnp.where(
            low_lane, dot(k_t[2 * p], both, ((1,), (1,))), dot(k_t[2 * p + 1], both, ((1,), (1,)))
        )

    half = rows // 2
    causal = lax.broadcasted_iota(jnp.int32, (half, half), 0) <= lax.broadcasted_iota(
        jnp.int32, (half, half), 1
    )

    def local(h, carry):
        def weigh(s_at, t_at, masked):
            scores = dot(k_t[h, :, s_at], q_t[h, :, t_at], ((0,), (0,)))
            weights = scores * scores * (1.0 / DH)
            if masked:
                weights = jnp.where(causal, weights, 0.0)
            total = jnp.sum(weights, axis=0, keepdims=True)
            return total, dot(v_t[h, :, s_at], weights.astype(jnp.bfloat16))

        low, high = slice(0, half), slice(half, rows)
        den_a, num_a = weigh(low, low, True)
        den_b, num_b = weigh(low, high, False)
        den_c, num_c = weigh(high, high, True)
        den[h, :, low] = den[h, :, low] + den_a
        den[h, :, high] = den[h, :, high] + (den_b + den_c)
        num[h, :, low] = num[h, :, low] + num_a
        num[h, :, high] = num[h, :, high] + (num_b + num_c)
        return carry

    def along(src, dst, send, recv, to):
        return pltpu.make_async_remote_copy(
            src_ref=src, dst_ref=dst, send_sem=send, recv_sem=recv,
            device_id=(to, hx), device_id_type=MESH,
        )

    def rs1_copy(line, i):
        return along(
            rs1_out.at[line, i], rs1_in.at[line, i], rs1_send.at[line, i], rs1_recv.at[line, i],
            sibling,
        )

    def rs2_copy(i):
        return along(rs2_out.at[i], rs2_in.at[i], rs2_send.at[i], rs2_recv.at[i], across_y)

    def chain_copy(i):
        return along(chain_out.at[i], chain_in.at[i], chain_send.at[i], chain_recv.at[i], above)

    def ag1_copy(i):
        return along(ag1_out.at[i], ag1_in.at[i], ag1_send.at[i], ag1_recv.at[i], across_y)

    def ag2_copy(line, i):
        return along(
            ag2_out.at[line, i], prefix.at[(2 * line + c) * parts + i], ag2_send.at[line, i],
            ag2_recv.at[line, i], sibling,
        )

    def wide(value):
        return value.astype(jnp.float32)

    def narrow(value):
        return value.astype(jnp.bfloat16)

    is_second_core, is_second_line = c.astype(jnp.float32), y.astype(jnp.float32)

    def make_unit(unit):
        if pairs >= GROUP:
            for j in range(pairs // GROUP):
                make_state(unit * (pairs // GROUP) + j)

    def give(line, unit):
        make_unit(unit)
        for i in range(parts):
            rs1_out[line, i] = narrow(state[unit * parts + i])
            rs1_copy(line, i).start()

    def settle(line, i, chip_prefix):
        at = (2 * line + c) * parts + i
        prefix[at] = narrow(chip_prefix + is_second_core * wide(rs1_in[line, i]))
        ag2_out[line, i] = narrow(chip_prefix + (1.0 - is_second_core) * state[at])
        ag2_copy(line, i).start()

    def own_part(i):
        rs1_copy(y, i).wait_recv()
        rs2_copy(i).wait_recv()

        @pl.when(z > 0)
        def _():
            chain_copy(i).wait_recv()

        mine = state[(2 * y + c) * parts + i] + wide(rs1_in[y, i])
        other = wide(rs2_in[i])
        before = wide(chain_in[i])

        @pl.when(z < planes - 1)
        def _():
            chain_out[i] = narrow(before + mine + other)
            chain_copy(i).start()

        ag1_out[i] = narrow(before + (1.0 - is_second_line) * mine)
        ag1_copy(i).start()
        settle(y, i, before + is_second_line * other)

    late = z >= planes // 2

    if pairs < GROUP:
        for p in range(pairs):
            make_state(p)
    far = 1 - y
    give(far, 2 * far + 1 - c)
    make_unit(2 * far + c)
    for i in range(parts):
        rs1_copy(far, i).wait_recv()
        rs2_out[i] = narrow(state[(2 * far + c) * parts + i] + wide(rs1_in[far, i]))
        rs2_copy(i).start()
    give(y, 2 * y + 1 - c)
    make_unit(2 * y + c)
    per = pairs // GROUP

    def fill(slot, spare, h):
        u = q_t[h]
        expand(slot, spare, u, u * (1.0 / DH), u * (2.0 / DH))

    def fill_far(core, carry):
        for j in range(per):
            for a in range(2):
                fill(2 + 2 * (per * core + j) + a, a, 2 * (per * (2 * far + core) + j) + a)
        return carry

    def own_step(i, carry):
        own_part(i)
        return local(i, carry)

    lax.fori_loop(0, jnp.where(late, 2, 0), fill_far, 0)
    lax.fori_loop(0, parts, own_step, 0)

    def far_parts():
        for i in range(parts):
            ag1_copy(i).wait_recv()
            settle(far, i, wide(ag1_in[i]))

    def query(p, slot, filled):
        whole = prefix[pl.ds(8 * p, 8)].reshape(ROWS, 2 * DH).T
        for a in range(2):
            h = 2 * p + a
            u = q_t[h]
            if not filled:
                fill(slot + a, a, h)
            mine = whole[a * DH:(a + 1) * DH, :]
            num[h] = num[h] + dot(mine[:, :FEATS], feat[slot + a])
            gram = dot(mine[:, FEATS:], u)
            den[h] = den[h] + jnp.sum(
                gram * u.astype(jnp.float32), axis=0, keepdims=True
            ) * (1.0 / DH)
        attended = jnp.concatenate(
            [num[2 * p + a] / (1.0 + den[2 * p + a]) for a in range(2)], axis=0
        )
        ss[0] = ss[0] + jnp.sum(attended * attended, axis=0, keepdims=True)
        gain = gain_mid_ref[:, pl.ds(pl.multiple_of(p * 2 * DH, 2 * DH), 2 * DH)]
        att[p] = (attended.T * gain.astype(jnp.float32)).astype(jnp.bfloat16)
        for k in range(1, nx):
            att_copy(k, p).start()

    if pairs >= GROUP:

        def near(step, carry):
            core = jnp.where(step == 0, c, 1 - c)

            @pl.when(step == 1)
            def _():
                for i in range(parts):
                    ag2_copy(y, i).wait_recv()

            for j in range(per):
                query((2 * y + core) * per + j, 0, False)
            return carry

        def distant(step, carry):
            core = jnp.where(step == 0, c, 1 - c)

            @pl.when(step == 1)
            def _():
                for i in range(parts):
                    ag2_copy(far, i).wait_recv()

            for j in range(per):
                query((2 * far + core) * per + j, 2 + 2 * (per * core + j), True)
            return carry

        lax.fori_loop(0, 2, near, 0)
        lax.fori_loop(0, jnp.where(late, 0, 2), fill_far, 0)
        far_parts()
        lax.fori_loop(0, 2, distant, 0)
    else:
        far_parts()
        for i in range(parts):
            for line in range(2):
                ag2_copy(line, i).wait_recv()
        for p in range(pairs):
            query(p, 0, False)
    for k in range(1, nx):
        ss_copy(k).start()
    own = pl.ds(pl.multiple_of(hx * width, width), width)
    update = jnp.zeros((rows, width), jnp.float32)
    for p in range(pairs):
        update = update + dot(att[p], wo_ref[p * 2 * DH:(p + 1) * 2 * DH, own])
    for k in range(1, nx):
        wo_copy(k).wait()
        for p in range(pairs):
            att_copy(k, p).wait()
            update = update + dot(att_in[k, p], wo_in[k, p * 2 * DH:(p + 1) * 2 * DH, :])
    for k in range(1, nx):
        ss_copy(k).wait()
    squares = ss[0]
    for k in range(1, nx):
        squares = squares + ss[k]
    columns = jnp.broadcast_to(squares[:1], (128, rows)).T[:, :1]
    scale = lax.rsqrt(columns / full + EPSILON)
    out_ref[...] = (x_own[...].astype(jnp.float32) + update * scale).astype(jnp.bfloat16)

    for i in range(parts):
        for line in range(2):
            rs1_copy(line, i).wait_send()
            ag2_copy(line, i).wait_send()
        rs2_copy(i).wait_send()
        ag1_copy(i).wait_send()

    @pl.when(z < planes - 1)
    def _():
        for i in range(parts):
            chain_copy(i).wait_send()


def shards(n, nx, tokens, w_qkv, w_out, gain_in, gain_mid):
    rows, width = tokens.shape
    features = w_qkv.shape[3]
    heads = features // DH
    pairs = heads // 2
    parts = 8 * pairs // GROUP
    bf16, f32 = jnp.bfloat16, jnp.float32
    dma = pltpu.SemaphoreType.DMA
    return pl.pallas_call(
        functools.partial(kernel, n, nx),
        out_shape=jax.ShapeDtypeStruct((rows, width), bf16),
        in_specs=[pl.BlockSpec(memory_space=pl.ANY)] * 3
        + [pl.BlockSpec(memory_space=pltpu.VMEM)] * 2,
        out_specs=pl.BlockSpec(memory_space=pltpu.VMEM),
        scratch_shapes=[
            pltpu.VMEM((rows, width), bf16),
            pltpu.VMEM((3, nx * width, features), bf16),
            pltpu.VMEM((features, nx * width), bf16),
            pltpu.VMEM((nx, features, width), bf16),
            pltpu.VMEM((nx, rows, width), bf16),
            pltpu.VMEM((heads, DH, rows), bf16),
            pltpu.VMEM((heads, DH, rows), bf16),
            pltpu.VMEM((heads, DH, rows), bf16),
            pltpu.VMEM((pairs, rows, 2 * DH), bf16),
            pltpu.VMEM((2 + 4 * (pairs // GROUP), FEATS, rows), bf16),
            pltpu.VMEM((2, rows // 128, 2 * DH, 128), f32),
            pltpu.VMEM((8 * pairs, PIECE, 2 * DH), f32),
            pltpu.VMEM((8 * pairs, PIECE, 2 * DH), bf16),
            pltpu.VMEM((2, parts, PIECE, 2 * DH), bf16),
            pltpu.VMEM((2, parts, PIECE, 2 * DH), bf16),
            pltpu.VMEM((parts, PIECE, 2 * DH), bf16),
            pltpu.VMEM((parts, PIECE, 2 * DH), bf16),
            pltpu.VMEM((parts, PIECE, 2 * DH), bf16),
            pltpu.VMEM((parts, PIECE, 2 * DH), bf16),
            pltpu.VMEM((parts, PIECE, 2 * DH), bf16),
            pltpu.VMEM((parts, PIECE, 2 * DH), bf16),
            pltpu.VMEM((2, parts, PIECE, 2 * DH), bf16),
            pltpu.VMEM((heads, DH, rows), f32),
            pltpu.VMEM((heads, 1, rows), f32),
            pltpu.VMEM((pairs, rows, 2 * DH), bf16),
            pltpu.VMEM((nx, pairs, rows, 2 * DH), bf16),
            pltpu.VMEM((nx, 8, rows), f32),
            dma((3,)),
            dma((nx, CHUNKS)), dma((nx, CHUNKS)),
            dma((nx,)), dma((nx,)),
            dma((2, parts)), dma((2, parts)),
            dma((parts,)), dma((parts,)),
            dma((parts,)), dma((parts,)),
            dma((parts,)), dma((parts,)),
            dma((2, parts)), dma((2, parts)),
            dma((nx,)), dma((nx,)),
            dma((nx, pairs)), dma((nx, pairs)),
        ],
        compiler_params=pltpu.CompilerParams(
            collective_id=0, has_side_effects=True, vmem_limit_bytes=60 * 1024 * 1024
        ),
    )(tokens, w_qkv[0].transpose(1, 0, 2), w_out[0], gain_in, gain_mid)


def solution(mesh):
    placed = (
        P("seq", "head"),
        P(None, None, None, "head"),
        P(None, "head", None),
        P(),
        P(None, "head"),
    )
    return jax.shard_map(
        functools.partial(shards, mesh.shape["seq"], mesh.shape["head"]),
        mesh=mesh, in_specs=placed, out_specs=P("seq", "head"), check_vma=False,
    )
```
